512 devices in a mesh: tok: 16 (over y_lo, x), voc: 32 (over y_hi, z, core).
Axes of the slice: x: 4, y: 8 (y_hi: 2, y_lo: 4; y = y_hi * 4 + y_lo), z: 8, core: 2. Of those that a mesh axis runs over, the one named last changes fastest.
Arguments:
- hidden: bfloat16 [8192, 1024], P('tok', 'voc'), may hold values from -6 to 6
- weight_values: bfloat16 [1024, 131072], P('tok', 'voc'), may hold values from -0.1875 to 0.1875
- scales: float32 [1024, 1024], P('tok', 'voc'), may hold values from 0.25 to 4
- partial_logits: bfloat16 [8192, 131072], P('tok', 'voc'), may hold values from -56 to 402
- targets: int32 [8192], P('tok'), may hold values from 0 to 131071
Outputs:
- loss: float32 [8192], P('tok')
The draws below stay inside these ranges and needn't reach their ends.
All inputs are finite; a program needn't handle non-finite values.
Results may differ from the reference program's by a relative error of at most 0.0015.
Values may be sent and summed in bfloat16 or wider, within the bound.
A program may use at most 128 MiB of HBM per device.

```python
import math
import jax
import jax.numpy as jnp
from jax import lax

V = 131072
SBLOCK = 128
KW = 1024
TOKENS = 8192


def draw_partial_logits(key, part):
    key = jax.random.fold_in(key, 11)
    keys = jax.random.split(key, 1)
    column = jnp.arange(V, dtype=jnp.int32)
    rise = 1.2 * column.astype(jnp.float32) / V
    base = jnp.clip(3.0 * jax.random.normal(keys[0], (TOKENS, V), jnp.float32), -18.0, 18.0)
    return (base + rise[None, :]).astype(jnp.bfloat16)


def with_ends(values, key, least, high):
    spot = [jax.random.randint(jax.random.fold_in(key, axis), (), 0, length) for axis, length in enumerate(values.shape)]
    widest = values.shape.index(max(values.shape))
    beside = spot[:widest] + [(spot[widest] + 1) % values.shape[widest]] + spot[widest + 1:]
    return values.at[tuple(spot)].set(least).at[tuple(beside)].set(high)


def level_of(stream_key, dims, cuts, smallest, high):
    gain = 1.0
    for position, parts in cuts:
        heights = jax.random.uniform(jax.random.fold_in(jax.random.fold_in(stream_key, 6), position), (parts,), jnp.float32, smallest / len(cuts), high / len(cuts))
        gain = gain * jnp.repeat(jnp.exp(heights), dims[position] // parts).reshape((-1,) + (1,) * (len(dims) - 1 - position))
    return gain


def scatter_about(rng, dims, spread, limit, pieces=(), kind=jnp.bfloat16):
    drawn = spread * jax.random.normal(rng, dims, jnp.float32)
    if pieces:
        drawn = drawn * level_of(rng, dims, pieces, -0.22, 0.18)
    return jnp.clip(drawn, -limit, limit).astype(kind)


def setup_inputs(seed: int = 0) -> dict:
    key_of = jax.random.split(jax.random.key(seed), 6)
    hidden = scatter_about(key_of[0], (TOKENS, KW), 1.0, 6.0, ((0, 16), (1, 32)))
    weight_values = scatter_about(key_of[1], (KW, V), KW ** -0.5, 0.1875, ((0, 16), (1, 32)))
    scales = jnp.clip(jnp.exp(math.log(4.0) - 2.7725887 * jax.random.uniform(key_of[2], (KW, V // SBLOCK), jnp.float32) ** level_of(key_of[2], (KW, V // SBLOCK), ((0, 16), (1, 32)), -0.2, 0.2)), 0.25, 4.0)
    partial_logits = draw_partial_logits(jax.random.fold_in(key_of[5], 71), 0)
    targets = with_ends(jax.random.randint(key_of[4], (TOKENS,), 0, V), jax.random.fold_in(key_of[4], 1), 0, V - 1).astype(jnp.int32)
    return dict(hidden=hidden, weight_values=weight_values, scales=scales, partial_logits=partial_logits, targets=targets)


def reference(hidden, weight_values, scales, partial_logits, targets):
    blocks_v = V // SBLOCK
    dense = (weight_values.astype(jnp.float32).reshape(KW, blocks_v, SBLOCK) * scales[:, :, None]).reshape(KW, V).astype(jnp.bfloat16)
    row_block = math.gcd(TOKENS, 256)
    count = TOKENS // row_block

    def one_block(items):
        rows_h, rows_p, rows_t = items
        full = rows_p.astype(jnp.float32) + jnp.dot(rows_h, dense, preferred_element_type=jnp.float32)
        top = jnp.max(full, axis=1)
        total = jnp.sum(jnp.exp(full - top[:, None]), axis=1)
        picked = jnp.take_along_axis(full, rows_t[:, None].astype(jnp.int32), axis=1)[:, 0]
        return top + jnp.log(total) - picked

    loss = lax.map(one_block, (hidden.reshape(count, row_block, KW), partial_logits.reshape(count, row_block, V), targets.reshape(count, row_block)))
    return loss.reshape(TOKENS)
```

```python
import functools

import jax
import jax.numpy as jnp
from jax import lax
from jax.experimental import pallas as pl
from jax.experimental.pallas import tpu as pltpu
from jax.sharding import PartitionSpec as P

MESH = pl.DeviceIdType.MESH
NX, NY, NZ = 4, 4, 8
ROWS, KLOC, VLOC, KSH, SB = 512, 64, 4096, 32, 128
QG = 7
QA = QG * SB
BC = VLOC - 4 * QA
BG = BC // SB
RC = 256
NRC = ROWS // RC


def kernel(
    hid_ref, w_ref, sc_ref, part_ref, tgt_ref, out_ref,
    ws, wa, wb, ht, hh, pa, pb, tg, tt, st, stb, sx, sv, sz,
    hy_s, hy_r, hx_s, hx_r, z_s, z_r, c_s, c_r, wax_s, wax_r, wbx_s, wbx_r,
    ya_s, ya_r, yb_s, yb_r, pa_s, pa_r, pa_l, pb_l, tg_s, tg_r, sx_s, sx_r, sv_s, sv_r, sz_s, sz_r,
):
    t_id, v_id = lax.axis_index("tok"), lax.axis_index("voc")
    x, y = lax.rem(t_id, NX), lax.div(t_id, NX)
    yh, z, c = lax.div(v_id, 16), lax.rem(lax.div(v_id, 2), NZ), lax.rem(v_id, 2)

    def dev(x_=None, y_=None, yh_=None, z_=None, c_=None):
        x_, y_ = x if x_ is None else x_, y if y_ is None else y_
        yh_, z_, c_ = yh if yh_ is None else yh_, z if z_ is None else z_, c if c_ is None else c_
        return (y_ * NX + x_, yh_ * 16 + z_ * 2 + c_)

    def xp(r):
        return lax.rem(x + r, NX)

    def xm(r):
        return lax.rem(x + NX - r, NX)

    def copy(src, dst, ss, rs, to):
        return pltpu.make_async_remote_copy(
            src_ref=src, dst_ref=dst, send_sem=ss, recv_sem=rs, device_id=to, device_id_type=MESH
        )

    bar = pltpu.get_barrier_semaphore()

    def greet(to):
        pl.semaphore_signal(bar, inc=1, device_id=to, device_id_type=MESH)

    for r in range(1, NX):
        greet(dev(x_=xp(r)))
    for r in range(1, NZ):
        greet(dev(z_=lax.rem(z + r, NZ)))
    for r in range(1, 4):
        greet(dev(yh_=lax.rem(yh + r // 2, 2), c_=lax.rem(c + r % 2, 2)))

    @pl.when(y > 0)
    def _():
        greet(dev(y_=y - 1))

    @pl.when(y < NY - 1)
    def _():
        greet(dev(y_=y + 1))

    own_pa = [
        pltpu.make_async_copy(
            part_ref.at[pl.ds(i * RC, RC), pl.ds(pl.multiple_of(x * QA, SB), QA)],
            pa.at[x, pl.ds(i * RC, RC)], pa_l.at[i],
        )
        for i in range(NRC)
    ]
    for d in own_pa:
        d.start()
    own_pb = pltpu.make_async_copy(part_ref.at[:, pl.ds(4 * QA, BC)], pb, pb_l)
    own_pb.start()

    def dense(g):
        scaled = w_ref[:, g * SB:(g + 1) * SB].astype(jnp.float32) * sc_ref[:, g:g + 1]
        return scaled.astype(jnp.bfloat16)

    for q in range(NX):
        for g in range(QG):
            ws[q, :, g * SB:(g + 1) * SB] = dense(q * QG + g)
    for g in range(BG):
        wb[t_id, :, g * SB:(g + 1) * SB] = dense(4 * QG + g)
    wa[t_id] = ws[x]
    eye = (
        lax.broadcasted_iota(jnp.int32, (KSH, KSH), 0) == lax.broadcasted_iota(jnp.int32, (KSH, KSH), 1)
    ).astype(jnp.bfloat16)
    ht[x, yh, z, c] = lax.dot_general(
        eye, hid_ref[...], (((1,), (1,)), ((), ())), preferred_element_type=jnp.float32
    ).astype(jnp.bfloat16)
    tg[x] = tgt_ref[...]

    near = jnp.where(y > 0, 1, 0) + jnp.where(y < NY - 1, 1, 0)
    pl.semaphore_wait(bar, (NX - 1) + (NZ - 1) + 3 + near)

    sends = []

    def start(d):
        d.start()
        sends.append(d)

    hy = copy(ht.at[x, yh, z, c], ht.at[x, yh, z, c], hy_s, hy_r, dev(yh_=1 - yh))
    start(hy)

    def hx(stream, r):
        ref = ht.at[x, yh if stream == 0 else 1 - yh, z, c]
        return copy(ref, ref, hx_s.at[stream, r], hx_r.at[stream, r], dev(x_=xp(r)))

    def hx_wait(stream, r):
        ref = ht.at[xm(r), yh if stream == 0 else 1 - yh, z, c]
        copy(ref, ref, hx_s.at[stream, r], hx_r.at[stream, r], dev(x_=xp(r))).wait_recv()

    order = (1, 3, 2)
    for r in order:
        start(hx(0, r))
    for r in order:
        start(copy(ws.at[xp(r)], wa.at[t_id], wax_s.at[r], wax_r.at[r], dev(x_=xp(r))))

    def ya_pass(s, r):
        src = wa_ref = None
        xs = xm(r)
        up = wa.at[jnp.maximum(y - s, 0) * NX + xs]
        down = wa.at[jnp.minimum(y + s, NY - 1) * NX + xs]
        cu = copy(up, up, ya_s.at[0, s, r], ya_r.at[0, s, r], dev(y_=jnp.minimum(y + 1, NY - 1)))
        cd = copy(down, down, ya_s.at[1, s, r], ya_r.at[1, s, r], dev(y_=jnp.maximum(y - 1, 0)))
        return cu, cd

    def go_up(s):
        return jnp.logical_and(y < NY - 1, y >= s)

    def go_down(s):
        return jnp.logical_and(y > 0, y + s <= NY - 1)

    def send_ya(s, r):
        cu, cd = ya_pass(s, r)

        @pl.when(go_up(s))
        def _():
            cu.start()

        @pl.when(go_down(s))
        def _():
            cd.start()

    def wait_ya(s, r):
        xs = xm(r)
        lo = wa.at[jnp.maximum(y - s - 1, 0) * NX + xs]
        hi = wa.at[jnp.minimum(y + s + 1, NY - 1) * NX + xs]

        @pl.when(y >= s + 1)
        def _():
            copy(lo, lo, ya_s.at[0, s, r], ya_r.at[0, s, r], dev()).wait_recv()

        @pl.when(y + s + 1 <= NY - 1)
        def _():
            copy(hi, hi, ya_s.at[1, s, r], ya_r.at[1, s, r], dev()).wait_recv()

    def yb_pass(s):
        up = wb.at[pl.ds(jnp.maximum(y - s, 0) * NX, NX)]
        down = wb.at[pl.ds(jnp.minimum(y + s, NY - 1) * NX, NX)]
        cu = copy(up, up, yb_s.at[0, s], yb_r.at[0, s], dev(y_=jnp.minimum(y + 1, NY - 1)))
        cd = copy(down, down, yb_s.at[1, s], yb_r.at[1, s], dev(y_=jnp.maximum(y - 1, 0)))
        return cu, cd

    def send_yb(s):
        cu, cd = yb_pass(s)

        @pl.when(go_up(s))
        def _():
            cu.start()

        @pl.when(go_down(s))
        def _():
            cd.start()

    def wait_yb(s):
        lo = wb.at[pl.ds(jnp.maximum(y - s - 1, 0) * NX, NX)]
        hi = wb.at[pl.ds(jnp.minimum(y + s + 1, NY - 1) * NX, NX)]

        @pl.when(y >= s + 1)
        def _():
            copy(lo, lo, yb_s.at[0, s], yb_r.at[0, s], dev()).wait_recv()

        @pl.when(y + s + 1 <= NY - 1)
        def _():
            copy(hi, hi, yb_s.at[1, s], yb_r.at[1, s], dev()).wait_recv()

    def zblock(stream, b):
        return ht.at[:, yh if stream == 0 else 1 - yh, b, c]

    def send_c(stream, j, b):
        ref = zblock(stream, b)
        start(copy(ref, ref, c_s.at[stream, j], c_r.at[stream, j], dev(c_=1 - c)))

    def send_z(stream, k):
        up, down = lax.rem(z + NZ - k, NZ), lax.rem(z + k, NZ)
        if k < 4:
            ref = zblock(stream, up)
            start(copy(ref, ref, z_s.at[stream, 0, k], z_r.at[stream, 0, k], dev(z_=lax.rem(z + 1, NZ))))
        if k < 3:
            ref = zblock(stream, down)
            start(copy(ref, ref, z_s.at[stream, 1, k], z_r.at[stream, 1, k], dev(z_=lax.rem(z + NZ - 1, NZ))))
        send_c(stream, k, up)
        if 0 < k < 4:
            send_c(stream, 4 + k, down)

    def wait_z(stream, k):
        up, down = lax.rem(z + NZ - k - 1, NZ), lax.rem(z + k + 1, NZ)
        if k < 4:
            ref = zblock(stream, up)
            copy(ref, ref, z_s.at[stream, 0, k], z_r.at[stream, 0, k], dev()).wait_recv()
        if k < 3:
            ref = zblock(stream, down)
            copy(ref, ref, z_s.at[stream, 1, k], z_r.at[stream, 1, k], dev()).wait_recv()

    def wait_c(stream):
        for j in range(NZ):
            b = lax.rem(z + NZ - j, NZ) if j <= 4 else lax.rem(z + j - 4, NZ)
            ref = ht.at[:, yh if stream == 0 else 1 - yh, b, 1 - c]
            copy(ref, ref, c_s.at[stream, j], c_r.at[stream, j], dev()).wait_recv()

    def pa_copy(r, i):
        src = part_ref.at[pl.ds(i * RC, RC), pl.ds(pl.multiple_of(xp(r) * QA, SB), QA)]
        return copy(src, pa.at[x, pl.ds(i * RC, RC)], pa_s.at[r, i], pa_r.at[r, i], dev(x_=xp(r)))

    send_ya(0, 0)
    for r in order:
        start(copy(wb.at[t_id], wb.at[t_id], wbx_s.at[r], wbx_r.at[r], dev(x_=xp(r))))
    for r in order:
        start(copy(tg.at[x], tg.at[x], tg_s.at[r], tg_r.at[r], dev(x_=xp(r))))

    def wax_wait(r):
        ref = wa.at[y * NX + xm(r)]
        copy(ref, ref, wax_s.at[r], wax_r.at[r], dev()).wait_recv()

    for r in order:
        hx_wait(0, r)
    send_z(0, 0)
    other = ht.at[x, 1 - yh, z, c]
    copy(other, other, hy_s, hy_r, dev()).wait_recv()
    for r in order:
        start(hx(1, r))
    for i in range(NRC):
        for r in order:
            start(pa_copy(r, i))
    for r in order:
        wax_wait(r)
        send_ya(0, r)
    wait_ya(0, 0)
    send_ya(1, 0)
    wait_z(0, 0)
    send_z(0, 1)
    for r in order:
        hx_wait(1, r)
    send_z(1, 0)
    wait_ya(0, 1)
    send_ya(1, 1)
    wait_ya(1, 0)
    send_ya(2, 0)
    wait_z(0, 1)
    send_z(0, 2)
    wait_ya(0, 3)
    send_ya(1, 3)
    wait_z(1, 0)
    send_z(1, 1)
    wait_ya(0, 2)
    send_ya(1, 2)
    wait_ya(1, 1)
    send_ya(2, 1)
    wait_z(0, 2)
    send_z(0, 3)
    wait_ya(1, 3)
    send_ya(2, 3)
    wait_z(1, 1)
    send_z(1, 2)
    wait_ya(1, 2)
    send_ya(2, 2)
    for r in order:
        ref = wb.at[y * NX + xm(r)]
        copy(ref, ref, wbx_s.at[r], wbx_r.at[r], dev()).wait_recv()
    send_yb(0)
    wait_z(0, 3)
    send_c(0, 4, lax.rem(z + 4, NZ))
    wait_z(1, 2)
    send_z(1, 3)
    for r in order:
        ref = tg.at[xm(r)]
        copy(ref, ref, tg_s.at[r], tg_r.at[r], dev()).wait_recv()

    def spread(i, carry):
        row = tg[i].astype(jnp.float32)
        tt[i] = jnp.broadcast_to(row, (SB, ROWS)).T
        return carry

    lax.fori_loop(0, NX, spread, 0)
    wait_yb(0)
    send_yb(1)
    wait_z(1, 3)
    send_c(1, 4, lax.rem(z + 4, NZ))
    wait_c(0)
    wait_c(1)

    def turn(i, carry):
        for kb in range(8):
            blk = ht[i, kb // 4, (kb % 4) * 2:(kb % 4) * 2 + 2].reshape(SB, ROWS)
            hh[i, :, kb * SB:(kb + 1) * SB] = blk.T
        return carry

    lax.fori_loop(0, NX, turn, 0)
    for r in (0, 1, 3, 2):
        wait_ya(2, r)

    def stats(logits, base, tcol):
        width = logits.shape[1]
        top = jnp.max(logits, axis=1, keepdims=True)
        lse = top + jnp.log(jnp.sum(jnp.exp(logits - top), axis=1, keepdims=True))
        col = lax.broadcasted_iota(jnp.int32, logits.shape, 1).astype(jnp.float32)
        want = tcol - base.astype(jnp.float32)
        hit = col == jnp.concatenate([want] * (width // SB), axis=1)
        pick = jnp.sum(jnp.where(hit, logits, 0.0), axis=1, keepdims=True)
        lane = lax.broadcasted_iota(jnp.int32, (logits.shape[0], SB), 1)
        both = jnp.where(lane == 0, lse, jnp.where(lane == 1, pick, 0.0))
        return both.T[0:2]

    def do_a(xs, row):
        rows = pl.ds(row, RC)
        logits = jnp.dot(
            hh[xs, rows, :], wa[...].reshape(NX * NY * KLOC, QA), preferred_element_type=jnp.float32
        ) + pa[xs, rows, :].astype(jnp.float32)
        st[xs, :, rows] = stats(logits, v_id * VLOC + x * QA, tt[xs, rows, :])

    def do_b(row):
        rows = pl.ds(row, RC)
        logits = jnp.dot(
            hh[x, rows, :], wb[...].reshape(NX * NY * KLOC, BC), preferred_element_type=jnp.float32
        ) + pb[rows, :].astype(jnp.float32)
        stb[:, rows] = stats(logits, v_id * VLOC + 4 * QA, tt[x, rows, :])

    for d in own_pa:
        d.wait()
    own_pb.wait()

    def part(j, carry):
        k = jnp.maximum(j - NRC, 0)
        i = jnp.where(j < NRC, j, lax.div(k, 3))
        r = jnp.where(j < NRC, 0, 1 + lax.rem(2 * lax.rem(k, 3), 3))
        xs = lax.rem(x + NX - r, NX)
        row = pl.multiple_of(i * RC, RC)

        @pl.when(j >= NRC)
        def _():
            ref = pa.at[xs, pl.ds(row, RC)]
            copy(ref, ref, pa_s.at[r, i], pa_r.at[r, i], dev()).wait_recv()

        do_a(xs, row)
        return carry

    lax.fori_loop(0, NRC + 3, part, 0)
    wait_yb(1)
    send_yb(2)
    lax.fori_loop(NRC + 3, NRC + 3 * NRC, part, 0)

    for r in order:
        start(copy(st.at[xp(r)], sx.at[x], sx_s.at[r], sx_r.at[r], dev(x_=xp(r))))
    sx[x] = st[x]
    wait_yb(2)

    def part_b(i, carry):
        do_b(pl.multiple_of(i * RC, RC))
        return carry

    lax.fori_loop(0, NRC, part_b, 0)
    for r in order:
        ref = sx.at[xm(r)]
        copy(ref, ref, sx_s.at[r], sx_r.at[r], dev()).wait_recv()

    def merge(rows):
        lses, picks = [a[0:1] for a in rows], [a[1:2] for a in rows]
        top = functools.reduce(jnp.maximum, lses)
        total = sum(jnp.exp(a - top) for a in lses)
        return top + jnp.log(total), sum(picks)

    g = yh * 2 + c
    lse, pick = merge([sx[i] for i in range(NX)] + [stb[...]])
    sv[g, 0:1] = lse
    sv[g, 1:2] = pick
    for r in range(1, 4):
        to = dev(yh_=lax.rem(yh + r // 2, 2), c_=lax.rem(c + r % 2, 2))
        start(copy(sv.at[g], sv.at[g], sv_s.at[r], sv_r.at[r], to))
    for r in range(1, 4):
        ref = sv.at[lax.rem(yh + r // 2, 2) * 2 + lax.rem(c + r % 2, 2)]
        copy(ref, ref, sv_s.at[r], sv_r.at[r], dev()).wait_recv()
    lse, pick = merge([sv[i] for i in range(4)])
    sz[z, 0:1] = lse
    sz[z, 1:2] = pick
    for r in (4, 3, 5, 2, 6, 1, 7):
        start(copy(sz.at[z], sz.at[z], sz_s.at[r], sz_r.at[r], dev(z_=lax.rem(z + r, NZ))))
    for r in (1, 7, 2, 6, 3, 5, 4):
        ref = sz.at[lax.rem(z + NZ - r, NZ)]
        copy(ref, ref, sz_s.at[r], sz_r.at[r], dev()).wait_recv()
    lse, pick = merge([sz[i] for i in range(NZ)])
    out_ref[...] = lse - pick

    for d in sends:
        d.wait_send()
    for s in range(3):
        for r in range(NX):
            cu, cd = ya_pass(s, r)

            @pl.when(go_up(s))
            def _():
                cu.wait_send()

            @pl.when(go_down(s))
            def _():
                cd.wait_send()

        bu, bd = yb_pass(s)

        @pl.when(go_up(s))
        def _():
            bu.wait_send()

        @pl.when(go_down(s))
        def _():
            bd.wait_send()


def on_device(hidden, weight_values, scales, partial_logits, targets):
    vmem = pl.BlockSpec(memory_space=pltpu.VMEM)
    dma = pltpu.SemaphoreType.DMA
    bf, f32 = jnp.bfloat16, jnp.float32
    n = NX * NY
    loss = pl.pallas_call(
        kernel,
        out_shape=jax.ShapeDtypeStruct((1, ROWS), f32),
        in_specs=[vmem, vmem, vmem, pl.BlockSpec(memory_space=pl.ANY), vmem],
        out_specs=vmem,
        scratch_shapes=[
            pltpu.VMEM((NX, KLOC, QA), bf),
            pltpu.VMEM((n, KLOC, QA), bf),
            pltpu.VMEM((n, KLOC, BC), bf),
            pltpu.VMEM((NX, 2, NZ, 2, KSH, ROWS), bf),
            pltpu.VMEM((NX, ROWS, n * KLOC), bf),
            pltpu.VMEM((NX, ROWS, QA), bf),
            pltpu.VMEM((ROWS, BC), bf),
            pltpu.VMEM((NX, 1, ROWS), jnp.int32),
            pltpu.VMEM((NX, ROWS, SB), f32),
            pltpu.VMEM((NX, 2, ROWS), f32),
            pltpu.VMEM((2, ROWS), f32),
            pltpu.VMEM((NX, 2, ROWS), f32),
            pltpu.VMEM((4, 2, ROWS), f32),
            pltpu.VMEM((NZ, 2, ROWS), f32),
            dma, dma, dma((2, 4)), dma((2, 4)), dma((2, 2, 4)), dma((2, 2, 4)), dma((2, 8)), dma((2, 8)),
            dma((4,)), dma((4,)), dma((4,)), dma((4,)),
            dma((2, 3, 4)), dma((2, 3, 4)), dma((2, 3)), dma((2, 3)),
            dma((4, NRC)), dma((4, NRC)), dma((NRC,)), dma,
            dma((4,)), dma((4,)), dma((4,)), dma((4,)), dma((4,)), dma((4,)), dma((8,)), dma((8,)),
        ],
        compiler_params=pltpu.CompilerParams(
            collective_id=0, has_side_effects=True, vmem_limit_bytes=48 << 20
        ),
    )(hidden, weight_values, scales, partial_logits, targets.reshape(1, ROWS))
    return loss.reshape(ROWS)


def solution(mesh):
    in_specs = (P("tok", "voc"), P("tok", "voc"), P("tok", "voc"), P("tok", "voc"), P("tok"))
    return jax.shard_map(on_device, mesh=mesh, in_specs=in_specs, out_specs=P("tok"), check_vma=False)
```

```python
import functools

import jax
import jax.numpy as jnp
from jax import lax
from jax.experimental import pallas as pl
from jax.experimental.pallas import tpu as pltpu
from jax.sharding import PartitionSpec as P

MESH = pl.DeviceIdType.MESH
NX, NY, NZ = 4, 4, 8
ROWS, KLOC, VLOC, KSH, SB = 512, 64, 4096, 32, 128
QG = 7
QA = QG * SB
BC = VLOC - 4 * QA
BG = BC // SB
RC = 256
NRC = ROWS // RC


def kernel(
    hid_ref, w_ref, sc_ref, part_ref, tgt_ref, out_ref,
    wv, scv, ws, wa, wb, ht, hh, pa, pb, tg, tt, st, stb, sx, sv, in_l,
    hy_s, hy_r, hx_s, hx_r, z_s, z_r, c_s, c_r, wax_s, wax_r, wbx_s, wbx_r,
    ya_s, ya_r, yb_s, yb_r, pa_s, pa_r, pa_l, pb_l, tg_s, tg_r, sx_s, sx_r, sv_s, sv_r,
):
    t_id, v_id = lax.axis_index("tok"), lax.axis_index("voc")
    x, y = lax.rem(t_id, NX), lax.div(t_id, NX)
    yh, z, c = lax.div(v_id, 16), lax.rem(lax.div(v_id, 2), NZ), lax.rem(v_id, 2)

    def dev(x_=None, y_=None, yh_=None, z_=None, c_=None):
        x_, y_ = x if x_ is None else x_, y if y_ is None else y_
        yh_, z_, c_ = yh if yh_ is None else yh_, z if z_ is None else z_, c if c_ is None else c_
        return (y_ * NX + x_, yh_ * 16 + z_ * 2 + c_)

    def xp(r):
        return lax.rem(x + r, NX)

    def xm(r):
        return lax.rem(x + NX - r, NX)

    def copy(src, dst, ss, rs, to):
        return pltpu.make_async_remote_copy(
            src_ref=src, dst_ref=dst, send_sem=ss, recv_sem=rs, device_id=to, device_id_type=MESH
        )

    bar = pltpu.get_barrier_semaphore()

    def greet(to):
        pl.semaphore_signal(bar, inc=1, device_id=to, device_id_type=MESH)

    for r in range(1, NX):
        greet(dev(x_=xp(r)))
    for r in range(1, NZ):
        greet(dev(z_=lax.rem(z + r, NZ)))
    for r in range(1, 4):
        greet(dev(yh_=lax.rem(yh + r // 2, 2), c_=lax.rem(c + r % 2, 2)))

    @pl.when(y > 0)
    def _():
        greet(dev(y_=y - 1))

    @pl.when(y < NY - 1)
    def _():
        greet(dev(y_=y + 1))

    loads = [
        pltpu.make_async_copy(w_ref, wv, in_l.at[0]),
        pltpu.make_async_copy(sc_ref, scv, in_l.at[1]),
        pltpu.make_async_copy(hid_ref, ht.at[x, yh, z, c], in_l.at[2]),
        pltpu.make_async_copy(tgt_ref, tg.at[x], in_l.at[3]),
    ]
    for d in loads:
        d.start()
    own_pa = [
        pltpu.make_async_copy(
            part_ref.at[pl.ds(i * RC, RC), pl.ds(pl.multiple_of(x * QA, SB), QA)],
            pa.at[x, pl.ds(i * RC, RC)], pa_l.at[i],
        )
        for i in range(NRC)
    ]
    for d in own_pa:
        d.start()
    own_pb = pltpu.make_async_copy(part_ref.at[:, pl.ds(4 * QA, BC)], pb, pb_l)
    own_pb.start()

    for d in loads:
        d.wait()
    sc = scv[...].T

    def dense(g):
        scaled = wv[:, g * SB:(g + 1) * SB].astype(jnp.float32) * sc[:, g:g + 1]
        return scaled.astype(jnp.bfloat16)

    for q in range(NX):
        for g in range(QG):
            ws[q, :, g * SB:(g + 1) * SB] = dense(q * QG + g)
    for g in range(BG):
        wb[t_id, :, g * SB:(g + 1) * SB] = dense(4 * QG + g)
    wa[t_id] = ws[x]

    near = jnp.where(y > 0, 1, 0) + jnp.where(y < NY - 1, 1, 0)
    pl.semaphore_wait(bar, (NX - 1) + (NZ - 1) + 3 + near)

    sends = []

    def start(d):
        d.start()
        sends.append(d)

    hy = copy(ht.at[x, yh, z, c], ht.at[x, yh, z, c], hy_s, hy_r, dev(yh_=1 - yh))
    start(hy)

    def hx(stream, r):
        ref = ht.at[x, yh if stream == 0 else 1 - yh, z, c]
        return copy(ref, ref, hx_s.at[stream, r], hx_r.at[stream, r], dev(x_=xp(r)))

    def hx_wait(stream, r):
        ref = ht.at[xm(r), yh if stream == 0 else 1 - yh, z, c]
        copy(ref, ref, hx_s.at[stream, r], hx_r.at[stream, r], dev(x_=xp(r))).wait_recv()

    order = (1, 3, 2)

    def ya_pass(s, r):
        xs = xm(r)
        up = wa.at[jnp.maximum(y - s, 0) * NX + xs]
        down = wa.at[jnp.minimum(y + s, NY - 1) * NX + xs]
        cu = copy(up, up, ya_s.at[0, s, r], ya_r.at[0, s, r], dev(y_=jnp.minimum(y + 1, NY - 1)))
        cd = copy(down, down, ya_s.at[1, s, r], ya_r.at[1, s, r], dev(y_=jnp.maximum(y - 1, 0)))
        return cu, cd

    def go_up(s):
        return jnp.logical_and(y < NY - 1, y >= s)

    def go_down(s):
        return jnp.logical_and(y > 0, y + s <= NY - 1)

    def send_ya(s, r):
        cu, cd = ya_pass(s, r)

        @pl.when(go_up(s))
        def _():
            cu.start()

        @pl.when(go_down(s))
        def _():
            cd.start()

    def wait_ya(s, r):
        xs = xm(r)
        lo = wa.at[jnp.maximum(y - s - 1, 0) * NX + xs]
        hi = wa.at[jnp.minimum(y + s + 1, NY - 1) * NX + xs]

        @pl.when(y >= s + 1)
        def _():
            copy(lo, lo, ya_s.at[0, s, r], ya_r.at[0, s, r], dev()).wait_recv()

        @pl.when(y + s + 1 <= NY - 1)
        def _():
            copy(hi, hi, ya_s.at[1, s, r], ya_r.at[1, s, r], dev()).wait_recv()

    def yb_pass(s):
        up = wb.at[pl.ds(jnp.maximum(y - s, 0) * NX, NX)]
        down = wb.at[pl.ds(jnp.minimum(y + s, NY - 1) * NX, NX)]
        cu = copy(up, up, yb_s.at[0, s], yb_r.at[0, s], dev(y_=jnp.minimum(y + 1, NY - 1)))
        cd = copy(down, down, yb_s.at[1, s], yb_r.at[1, s], dev(y_=jnp.maximum(y - 1, 0)))
        return cu, cd

    def send_yb(s):
        cu, cd = yb_pass(s)

        @pl.when(go_up(s))
        def _():
            cu.start()

        @pl.when(go_down(s))
        def _():
            cd.start()

    def wait_yb(s):
        lo = wb.at[pl.ds(jnp.maximum(y - s - 1, 0) * NX, NX)]
        hi = wb.at[pl.ds(jnp.minimum(y + s + 1, NY - 1) * NX, NX)]

        @pl.when(y >= s + 1)
        def _():
            copy(lo, lo, yb_s.at[0, s], yb_r.at[0, s], dev()).wait_recv()

        @pl.when(y + s + 1 <= NY - 1)
        def _():
            copy(hi, hi, yb_s.at[1, s], yb_r.at[1, s], dev()).wait_recv()

    def zblock(stream, b):
        return ht.at[:, yh if stream == 0 else 1 - yh, b, c]

    def send_c(stream, j, b):
        ref = zblock(stream, b)
        start(copy(ref, ref, c_s.at[stream, j], c_r.at[stream, j], dev(c_=1 - c)))

    def send_z(stream, k):
        up, down = lax.rem(z + NZ - k, NZ), lax.rem(z + k, NZ)
        if k < 4:
            ref = zblock(stream, up)
            start(copy(ref, ref, z_s.at[stream, 0, k], z_r.at[stream, 0, k], dev(z_=lax.rem(z + 1, NZ))))
        if k < 3:
            ref = zblock(stream, down)
            start(copy(ref, ref, z_s.at[stream, 1, k], z_r.at[stream, 1, k], dev(z_=lax.rem(z + NZ - 1, NZ))))
        send_c(stream, k, up)
        if 0 < k < 4:
            send_c(stream, 4 + k, down)

    def wait_z(stream, k):
        up, down = lax.rem(z + NZ - k - 1, NZ), lax.rem(z + k + 1, NZ)
        if k < 4:
            ref = zblock(stream, up)
            copy(ref, ref, z_s.at[stream, 0, k], z_r.at[stream, 0, k], dev()).wait_recv()
        if k < 3:
            ref = zblock(stream, down)
            copy(ref, ref, z_s.at[stream, 1, k], z_r.at[stream, 1, k], dev()).wait_recv()

    def wait_c(stream):
        for j in range(NZ):
            b = lax.rem(z + NZ - j, NZ) if j <= 4 else lax.rem(z + j - 4, NZ)
            ref = ht.at[:, yh if stream == 0 else 1 - yh, b, 1 - c]
            copy(ref, ref, c_s.at[stream, j], c_r.at[stream, j], dev()).wait_recv()

    def pa_copy(r, i):
        src = part_ref.at[pl.ds(i * RC, RC), pl.ds(pl.multiple_of(xp(r) * QA, SB), QA)]
        return copy(src, pa.at[x, pl.ds(i * RC, RC)], pa_s.at[r, i], pa_r.at[r, i], dev(x_=xp(r)))

    def wax_wait(r):
        ref = wa.at[y * NX + xm(r)]
        copy(ref, ref, wax_s.at[r], wax_r.at[r], dev()).wait_recv()

    def turn(stream):
        half = yh if stream == 0 else 1 - yh

        def one(i, carry):
            for kb in range(4):
                blk = ht[i, half, kb * 2:kb * 2 + 2].reshape(SB, ROWS)
                hh[i, :, pl.ds(pl.multiple_of(half * 4 * SB, SB) + kb * SB, SB)] = blk.T
            return carry

        lax.fori_loop(0, NX, one, 0)

    for r in order:
        start(hx(0, r))
    send_ya(0, 0)
    for r in order:
        start(copy(ws.at[xp(r)], wa.at[t_id], wax_s.at[r], wax_r.at[r], dev(x_=xp(r))))
    for r in order:
        hx_wait(0, r)
    send_z(0, 0)
    other = ht.at[x, 1 - yh, z, c]
    copy(other, other, hy_s, hy_r, dev()).wait_recv()
    for r in order:
        start(hx(1, r))
    for r in order:
        start(copy(wb.at[t_id], wb.at[t_id], wbx_s.at[r], wbx_r.at[r], dev(x_=xp(r))))
    for r in order:
        start(copy(tg.at[x], tg.at[x], tg_s.at[r], tg_r.at[r], dev(x_=xp(r))))
    for i in range(NRC):
        for r in (2, 1, 3):
            start(pa_copy(r, i))
    wax_wait(1)
    send_ya(0, 1)
    wax_wait(3)
    send_ya(0, 3)
    wait_ya(0, 0)
    send_ya(1, 0)
    wax_wait(2)
    send_ya(0, 2)
    wait_z(0, 0)
    send_z(0, 1)
    for r in order:
        hx_wait(1, r)
    send_z(1, 0)
    wait_ya(0, 1)
    send_ya(1, 1)
    wait_ya(1, 0)
    send_ya(2, 0)
    wait_z(0, 1)
    send_z(0, 2)
    wait_z(1, 0)
    send_z(1, 1)
    wait_ya(0, 3)
    send_ya(1, 3)
    wait_ya(1, 1)
    send_ya(2, 1)
    wait_ya(0, 2)
    send_ya(1, 2)
    wait_z(0, 2)
    send_z(0, 3)
    wait_z(1, 1)
    send_z(1, 2)
    wait_ya(1, 3)
    send_ya(2, 3)
    wait_ya(1, 2)
    send_ya(2, 2)
    for r in order:
        ref = wb.at[y * NX + xm(r)]
        copy(ref, ref, wbx_s.at[r], wbx_r.at[r], dev()).wait_recv()
    send_yb(0)
    wait_z(0, 3)
    send_c(0, 4, lax.rem(z + 4, NZ))
    wait_z(1, 2)
    send_z(1, 3)

    for r in order:
        ref = tg.at[xm(r)]
        copy(ref, ref, tg_s.at[r], tg_r.at[r], dev()).wait_recv()

    def spread(i, carry):
        row = tg[i].astype(jnp.float32)
        tt[i] = jnp.broadcast_to(row, (SB, ROWS)).T
        return carry

    lax.fori_loop(0, NX, spread, 0)
    wait_c(0)
    turn(0)
    wait_yb(0)
    send_yb(1)
    wait_z(1, 3)
    send_c(1, 4, lax.rem(z + 4, NZ))
    wait_c(1)
    turn(1)
    for r in (0, 1, 3, 2):
        wait_ya(2, r)

    def stats(logits, base, tcol):
        width = logits.shape[1]
        top = jnp.max(logits, axis=1, keepdims=True)
        lse = top + jnp.log(jnp.sum(jnp.exp(logits - top), axis=1, keepdims=True))
        col = lax.broadcasted_iota(jnp.int32, logits.shape, 1).astype(jnp.float32)
        want = tcol - base.astype(jnp.float32)
        hit = col == jnp.concatenate([want] * (width // SB), axis=1)
        pick = jnp.sum(jnp.where(hit, logits, 0.0), axis=1, keepdims=True)
        lane = lax.broadcasted_iota(jnp.int32, (logits.shape[0], SB), 1)
        both = jnp.where(lane == 0, lse, jnp.where(lane == 1, pick, 0.0))
        return both.T[0:2]

    def do_a(xs, row):
        rows = pl.ds(row, RC)
        logits = jnp.dot(
            hh[xs, rows, :], wa[...].reshape(NX * NY * KLOC, QA), preferred_element_type=jnp.float32
        ) + pa[xs, rows, :].astype(jnp.float32)
        st[xs, :, rows] = stats(logits, v_id * VLOC + x * QA, tt[xs, rows, :])

    def do_b(row):
        rows = pl.ds(row, RC)
        logits = jnp.dot(
            hh[x, rows, :], wb[...].reshape(NX * NY * KLOC, BC), preferred_element_type=jnp.float32
        ) + pb[rows, :].astype(jnp.float32)
        stb[:, rows] = stats(logits, v_id * VLOC + 4 * QA, tt[x, rows, :])

    for d in own_pa:
        d.wait()
    own_pb.wait()

    def sx_copy(r):
        to = lax.rem(x + NX - r, NX)
        return copy(st.at[to], sx.at[x], sx_s.at[NX - r], sx_r.at[NX - r], dev(x_=to))

    def part(j, carry):
        k = jnp.maximum(j - NRC, 0)
        i = jnp.where(j < NRC, j, lax.div(k, 3))
        r = jnp.where(j < NRC, 0, 1 + lax.rem(lax.rem(k, 3) + 1, 3))
        xs = lax.rem(x + NX - r, NX)
        row = pl.multiple_of(i * RC, RC)

        @pl.when(j >= NRC)
        def _():
            ref = pa.at[xs, pl.ds(row, RC)]
            copy(ref, ref, pa_s.at[r, i], pa_r.at[r, i], dev()).wait_recv()

        do_a(xs, row)

        @pl.when(j >= NRC + 3 * (NRC - 1))
        def _():
            sx_copy(r).start()

        return carry

    lax.fori_loop(0, NRC + 3, part, 0)
    wait_yb(1)
    send_yb(2)
    lax.fori_loop(NRC + 3, NRC + 3 * NRC, part, 0)

    sends.extend(sx_copy(r) for r in order)
    sx[x] = st[x]
    wait_yb(2)

    def part_b(i, carry):
        do_b(pl.multiple_of(i * RC, RC))
        return carry

    lax.fori_loop(0, NRC, part_b, 0)
    for r in order:
        ref = sx.at[xm(r)]
        copy(ref, ref, sx_s.at[r], sx_r.at[r], dev()).wait_recv()

    def merge(rows):
        lses, picks = [a[0:1] for a in rows], [a[1:2] for a in rows]
        top = functools.reduce(jnp.maximum, lses)
        total = sum(jnp.exp(a - top) for a in lses)
        return top + jnp.log(total), sum(picks)

    lse, pick = merge([sx[i] for i in range(NX)] + [stb[...]])
    sv[v_id, 0:1] = lse
    sv[v_id, 1:2] = pick

    def peer(i, sign):
        dz = (4, 3, 5, 2, 6, 1, 7, 0)[i // 4]
        return (
            lax.rem(yh + 1 - i % 4 // 2, 2), lax.rem(z + NZ + sign * dz, NZ), lax.rem(c + 1 - i % 2, 2)
        )

    for i in range(31):
        to = peer(i, 1)
        start(copy(sv.at[v_id], sv.at[v_id], sv_s.at[i], sv_r.at[i], dev(yh_=to[0], z_=to[1], c_=to[2])))
    for d in sends:
        d.wait_send()
    for s in range(3):
        for r in range(NX):
            cu, cd = ya_pass(s, r)

            @pl.when(go_up(s))
            def _():
                cu.wait_send()

            @pl.when(go_down(s))
            def _():
                cd.wait_send()

        bu, bd = yb_pass(s)

        @pl.when(go_up(s))
        def _():
            bu.wait_send()

        @pl.when(go_down(s))
        def _():
            bd.wait_send()
    for i in range(30, -1, -1):
        a_, b_, c_ = peer(i, -1)
        ref = sv.at[a_ * 16 + b_ * 2 + c_]
        copy(ref, ref, sv_s.at[i], sv_r.at[i], dev()).wait_recv()
    every = sv[...]
    lses, picks = every[:, 0, :], every[:, 1, :]
    top = jnp.max(lses, axis=0, keepdims=True)
    total = jnp.sum(jnp.exp(lses - top), axis=0, keepdims=True)
    out_ref[...] = top + jnp.log(total) - jnp.sum(picks, axis=0, keepdims=True)


def on_device(hidden, weight_values, scales, partial_logits, targets):
    vmem = pl.BlockSpec(memory_space=pltpu.VMEM)
    dma = pltpu.SemaphoreType.DMA
    bf, f32 = jnp.bfloat16, jnp.float32
    n = NX * NY
    loss = pl.pallas_call(
        kernel,
        out_shape=jax.ShapeDtypeStruct((1, ROWS), f32),
        in_specs=[pl.BlockSpec(memory_space=pltpu.HBM)] * 5,
        out_specs=vmem,
        scratch_shapes=[
            pltpu.VMEM((KLOC, VLOC), bf),
            pltpu.VMEM((VLOC // SB, KLOC), f32),
            pltpu.VMEM((NX, KLOC, QA), bf),
            pltpu.VMEM((n, KLOC, QA), bf),
            pltpu.VMEM((n, KLOC, BC), bf),
            pltpu.VMEM((NX, 2, NZ, 2, KSH, ROWS), bf),
            pltpu.VMEM((NX, ROWS, n * KLOC), bf),
            pltpu.VMEM((NX, ROWS, QA), bf),
            pltpu.VMEM((ROWS, BC), bf),
            pltpu.VMEM((NX, 1, ROWS), jnp.int32),
            pltpu.VMEM((NX, ROWS, SB), f32),
            pltpu.VMEM((NX, 2, ROWS), f32),
            pltpu.VMEM((2, ROWS), f32),
            pltpu.VMEM((NX, 2, ROWS), f32),
            pltpu.VMEM((32, 2, ROWS), f32),
            dma((4,)),
            dma, dma, dma((2, 4)), dma((2, 4)), dma((2, 2, 4)), dma((2, 2, 4)), dma((2, 8)), dma((2, 8)),
            dma((4,)), dma((4,)), dma((4,)), dma((4,)),
            dma((2, 3, 4)), dma((2, 3, 4)), dma((2, 3)), dma((2, 3)),
            dma((4, NRC)), dma((4, NRC)), dma((NRC,)), dma,
            dma((4,)), dma((4,)), dma((4,)), dma((4,)), dma((31,)), dma((31,)),
        ],
        compiler_params=pltpu.CompilerParams(
            collective_id=0, has_side_effects=True, vmem_limit_bytes=60 << 20
        ),
    )(hidden.T, weight_values, scales.T, partial_logits, targets.reshape(1, ROWS))
    return loss.reshape(ROWS)


def solution(mesh):
    in_specs = (P("tok", "voc"), P("tok", "voc"), P("tok", "voc"), P("tok", "voc"), P("tok"))
    return jax.shard_map(on_device, mesh=mesh, in_specs=in_specs, out_specs=P("tok"), check_vma=False)
```

```python
import functools

import jax
import jax.numpy as jnp
from jax import lax
from jax.experimental import pallas as pl
from jax.experimental.pallas import tpu as pltpu
from jax.sharding import PartitionSpec as P

MESH = pl.DeviceIdType.MESH
NX, NY, NZ = 4, 4, 8
ROWS, KLOC, VLOC, KSH, SB = 512, 64, 4096, 32, 128
QG = 6
QA = QG * SB
BG = VLOC // SB // NX - QG
QB = BG * SB
B0 = NX * QA
RC = 256
NRC = ROWS // RC


def kernel(
    hid_ref, w_ref, sc_ref, part_ref, tgt_ref, out_ref,
    wv, scv, ws, wsb, wa, wb, ht, hh, pa, pb, pc, tg, tt, st, stb, sx, sv, in_l,
    hy_s, hy_r, hx_s, hx_r, z_s, z_r, c_s, c_r, wax_s, wax_r, wbx_s, wbx_r,
    ya_s, ya_r, yb_s, yb_r, pa_s, pa_r, pb_s, pb_r, pa_l, pb_l, tg_s, tg_r, sx_s, sx_r, sv_s, sv_r,
):
    t_id, v_id = lax.axis_index("tok"), lax.axis_index("voc")
    x, y = lax.rem(t_id, NX), lax.div(t_id, NX)
    yh, z, c = lax.div(v_id, 16), lax.rem(lax.div(v_id, 2), NZ), lax.rem(v_id, 2)

    def dev(x_=None, y_=None, yh_=None, z_=None, c_=None):
        x_, y_ = x if x_ is None else x_, y if y_ is None else y_
        yh_, z_, c_ = yh if yh_ is None else yh_, z if z_ is None else z_, c if c_ is None else c_
        return (y_ * NX + x_, yh_ * 16 + z_ * 2 + c_)

    def xp(r):
        return lax.rem(x + r, NX)

    def xm(r):
        return lax.rem(x + NX - r, NX)

    def copy(src, dst, ss, rs, to):
        return pltpu.make_async_remote_copy(
            src_ref=src, dst_ref=dst, send_sem=ss, recv_sem=rs, device_id=to, device_id_type=MESH
        )

    bar = pltpu.get_barrier_semaphore()

    def greet(to):
        pl.semaphore_signal(bar, inc=1, device_id=to, device_id_type=MESH)

    for r in range(1, NX):
        greet(dev(x_=xp(r)))
    for r in range(1, NZ):
        greet(dev(z_=lax.rem(z + r, NZ)))
    for r in range(1, 4):
        greet(dev(yh_=lax.rem(yh + r // 2, 2), c_=lax.rem(c + r % 2, 2)))

    @pl.when(y > 0)
    def _():
        greet(dev(y_=y - 1))

    @pl.when(y < NY - 1)
    def _():
        greet(dev(y_=y + 1))

    loads = [
        pltpu.make_async_copy(w_ref, wv, in_l.at[0]),
        pltpu.make_async_copy(sc_ref, scv, in_l.at[1]),
        pltpu.make_async_copy(hid_ref, ht.at[x, yh, z, c], in_l.at[2]),
        pltpu.make_async_copy(tgt_ref, tg.at[x], in_l.at[3]),
    ]
    for d in loads:
        d.start()
    own_pa = [
        pltpu.make_async_copy(
            part_ref.at[pl.ds(i * RC, RC), pl.ds(pl.multiple_of(x * QA, SB), QA)],
            pa.at[x, pl.ds(i * RC, RC)], pa_l.at[i],
        )
        for i in range(NRC)
    ]
    for d in own_pa:
        d.start()
    far = xp(2)
    own_pb = [
        pltpu.make_async_copy(
            part_ref.at[:, pl.ds(pl.multiple_of(B0 + q * QB, SB), QB)], dst, pb_l.at[i]
        )
        for i, (q, dst) in enumerate(((x, pb.at[x]), (far, pc)))
    ]
    for d in own_pb:
        d.start()

    near = jnp.where(y > 0, 1, 0) + jnp.where(y < NY - 1, 1, 0)
    pl.semaphore_wait(bar, (NX - 1) + (NZ - 1) + 3 + near)
    loads[2].wait()

    sends = []

    def start(d):
        d.start()
        sends.append(d)

    def hx(r):
        ref = ht.at[x, yh, z, c]
        return copy(ref, ref, hx_s.at[r], hx_r.at[r], dev(x_=xp(r)))

    def hx_wait(r):
        ref = ht.at[xm(r), yh, z, c]
        copy(ref, ref, hx_s.at[r], hx_r.at[r], dev(x_=xp(r))).wait_recv()

    order = (1, 3, 2)

    def ya_pass(s, r):
        xs = xm(r)
        up = wa.at[jnp.maximum(y - s, 0) * NX + xs]
        down = wa.at[jnp.minimum(y + s, NY - 1) * NX + xs]
        cu = copy(up, up, ya_s.at[0, s, r], ya_r.at[0, s, r], dev(y_=jnp.minimum(y + 1, NY - 1)))
        cd = copy(down, down, ya_s.at[1, s, r], ya_r.at[1, s, r], dev(y_=jnp.maximum(y - 1, 0)))
        return cu, cd

    def go_up(s):
        return jnp.logical_and(y < NY - 1, y >= s)

    def go_down(s):
        return jnp.logical_and(y > 0, y + s <= NY - 1)

    def send_ya(s, r):
        cu, cd = ya_pass(s, r)

        @pl.when(go_up(s))
        def _():
            cu.start()

        @pl.when(go_down(s))
        def _():
            cd.start()

    def wait_ya(s, r):
        xs = xm(r)
        lo = wa.at[jnp.maximum(y - s - 1, 0) * NX + xs]
        hi = wa.at[jnp.minimum(y + s + 1, NY - 1) * NX + xs]

        @pl.when(y >= s + 1)
        def _():
            copy(lo, lo, ya_s.at[0, s, r], ya_r.at[0, s, r], dev()).wait_recv()

        @pl.when(y + s + 1 <= NY - 1)
        def _():
            copy(hi, hi, ya_s.at[1, s, r], ya_r.at[1, s, r], dev()).wait_recv()

    def yb_pass(p, s):
        up = wb.at[p, pl.ds(jnp.maximum(y - s, 0) * NX, NX)]
        down = wb.at[p, pl.ds(jnp.minimum(y + s, NY - 1) * NX, NX)]
        cu = copy(up, up, yb_s.at[p, 0, s], yb_r.at[p, 0, s], dev(y_=jnp.minimum(y + 1, NY - 1)))
        cd = copy(down, down, yb_s.at[p, 1, s], yb_r.at[p, 1, s], dev(y_=jnp.maximum(y - 1, 0)))
        return cu, cd

    def send_yb(p, s):
        cu, cd = yb_pass(p, s)

        @pl.when(go_up(s))
        def _():
            cu.start()

        @pl.when(go_down(s))
        def _():
            cd.start()

    def wait_yb(p, s):
        lo = wb.at[p, pl.ds(jnp.maximum(y - s - 1, 0) * NX, NX)]
        hi = wb.at[p, pl.ds(jnp.minimum(y + s + 1, NY - 1) * NX, NX)]

        @pl.when(y >= s + 1)
        def _():
            copy(lo, lo, yb_s.at[p, 0, s], yb_r.at[p, 0, s], dev()).wait_recv()

        @pl.when(y + s + 1 <= NY - 1)
        def _():
            copy(hi, hi, yb_s.at[p, 1, s], yb_r.at[p, 1, s], dev()).wait_recv()

    def zblock(stream, b):
        return ht.at[:, yh if stream == 0 else 1 - yh, b, c]

    def zhalf(stream, h, b):
        return ht.at[2 * h:2 * h + 2, yh if stream == 0 else 1 - yh, b, c]

    def zcopy(stream, h, way, k, b, to):
        ref = zhalf(stream, h, b)
        return copy(ref, ref, z_s.at[stream, h, way, k], z_r.at[stream, h, way, k], to)

    def send_c(stream, j, b):
        ref = zblock(stream, b)
        start(copy(ref, ref, c_s.at[stream, j], c_r.at[stream, j], dev(c_=1 - c)))

    def send_z(stream, k):
        up, down = lax.rem(z + NZ - k, NZ), lax.rem(z + k, NZ)
        for h in range(2):
            if k < 4 - h:
                start(zcopy(stream, h, 0, k, up, dev(z_=lax.rem(z + 1, NZ))))
            if k < 3 + h:
                start(zcopy(stream, h, 1, k, down, dev(z_=lax.rem(z + NZ - 1, NZ))))
        send_c(stream, k, up)
        if 0 < k < 4:
            send_c(stream, 4 + k, down)

    def step_z(stream, k):
        up, down = lax.rem(z + NZ - k - 1, NZ), lax.rem(z + k + 1, NZ)
        for h in range(2):
            if k < 4 - h:
                zcopy(stream, h, 0, k, up, dev()).wait_recv()
            if k < 3 + h:
                zcopy(stream, h, 1, k, down, dev()).wait_recv()
        if k < 3:
            send_z(stream, k + 1)
        else:
            send_c(stream, 4, up)

    def wait_c(stream):
        for j in range(NZ):
            b = lax.rem(z + NZ - j, NZ) if j <= 4 else lax.rem(z + j - 4, NZ)
            ref = ht.at[:, yh if stream == 0 else 1 - yh, b, 1 - c]
            copy(ref, ref, c_s.at[stream, j], c_r.at[stream, j], dev()).wait_recv()

    def pa_copy(r, i):
        src = part_ref.at[pl.ds(i * RC, RC), pl.ds(pl.multiple_of(xp(r) * QA, SB), QA)]
        return copy(src, pa.at[x, pl.ds(i * RC, RC)], pa_s.at[r, i], pa_r.at[r, i], dev(x_=xp(r)))

    def pb_copy(r, i):
        src = part_ref.at[pl.ds(i * RC, RC), pl.ds(pl.multiple_of(B0 + xp(r) * QB, SB), QB)]
        return copy(src, pb.at[x, pl.ds(i * RC, RC)], pb_s.at[r, i], pb_r.at[r, i], dev(x_=xp(r)))

    def wbx_wait(p):
        for r in order:
            ref = wb.at[p, y * NX + xm(r)]
            copy(ref, ref, wbx_s.at[p, r], wbx_r.at[p, r], dev()).wait_recv()

    def wax_wait(r):
        ref = wa.at[y * NX + xm(r)]
        copy(ref, ref, wax_s.at[r], wax_r.at[r], dev()).wait_recv()

    def turn(stream):
        half = yh if stream == 0 else 1 - yh

        def one(i, carry):
            for kb in range(4):
                blk = ht[i, half, kb * 2:kb * 2 + 2].reshape(SB, ROWS)
                hh[i, :, pl.ds(pl.multiple_of(half * 4 * SB, SB) + kb * SB, SB)] = blk.T
            return carry

        lax.fori_loop(0, NX, one, 0)

    def send_wb(p):
        for r in order:
            start(copy(wsb.at[xp(r + 2 * p)], wb.at[p, t_id], wbx_s.at[p, r], wbx_r.at[p, r], dev(x_=xp(r))))

    def pass_ya(s, r):
        wait_ya(s - 1, r)
        send_ya(s, r)

    def pass_yb(p, s):
        wait_yb(p, s - 1)
        send_yb(p, s)

    for r in order:
        start(hx(r))

    for i in (0, 1, 3):
        loads[i].wait()
    sc = scv[...].T

    def dense(g):
        scaled = wv[:, g * SB:(g + 1) * SB].astype(jnp.float32) * sc[:, g:g + 1]
        return scaled.astype(jnp.bfloat16)

    for q in range(NX):
        for g in range(QG):
            ws[q, :, g * SB:(g + 1) * SB] = dense(q * QG + g)
        for g in range(BG):
            wsb[q, :, g * SB:(g + 1) * SB] = dense(NX * QG + q * BG + g)
    wa[t_id] = ws[x]
    wb[0, t_id] = wsb[x]
    wb[1, t_id] = wsb[far]

    send_ya(0, 0)
    for r in order:
        start(copy(ws.at[xp(r)], wa.at[t_id], wax_s.at[r], wax_r.at[r], dev(x_=xp(r))))
    send_wb(0)
    send_wb(1)
    for r in order:
        start(copy(tg.at[x], tg.at[x], tg_s.at[r], tg_r.at[r], dev(x_=xp(r))))
    for i in range(NRC):
        for r in (2, 1, 3):
            start(pa_copy(r, i))
    for i in range(NRC):
        for r in (1, 3):
            start(pb_copy(r, i))
    for r in order:
        hx_wait(r)
    send_z(0, 0)
    ref = zblock(0, z)
    start(copy(ref, ref, hy_s, hy_r, dev(yh_=1 - yh)))
    wax_wait(1)
    send_ya(0, 1)
    wax_wait(3)
    send_ya(0, 3)
    pass_ya(1, 0)
    wax_wait(2)
    send_ya(0, 2)
    step_z(0, 0)
    ref = zblock(1, z)
    copy(ref, ref, hy_s, hy_r, dev()).wait_recv()
    send_z(1, 0)
    pass_ya(1, 1)
    pass_ya(2, 0)
    pass_ya(1, 3)
    pass_ya(1, 2)
    step_z(0, 1)
    wbx_wait(0)
    send_yb(0, 0)
    step_z(1, 0)
    pass_ya(2, 1)
    pass_ya(2, 3)
    step_z(0, 2)
    pass_ya(2, 2)
    step_z(1, 1)
    wbx_wait(1)
    send_yb(1, 0)
    step_z(0, 3)
    step_z(1, 2)
    pass_yb(0, 1)

    for r in order:
        ref = tg.at[xm(r)]
        copy(ref, ref, tg_s.at[r], tg_r.at[r], dev()).wait_recv()

    def spread(i, carry):
        row = tg[i].astype(jnp.float32)
        tt[i] = jnp.broadcast_to(row, (SB, ROWS)).T
        return carry

    lax.fori_loop(0, NX, spread, 0)
    wait_c(0)
    turn(0)
    step_z(1, 3)
    pass_yb(1, 1)
    wait_c(1)
    turn(1)
    for r in (0, 1, 3, 2):
        wait_ya(2, r)

    def stats(logits, base, tcol):
        width = logits.shape[1]
        top = jnp.max(logits, axis=1, keepdims=True)
        lse = top + jnp.log(jnp.sum(jnp.exp(logits - top), axis=1, keepdims=True))
        col = lax.broadcasted_iota(jnp.int32, logits.shape, 1).astype(jnp.float32)
        want = tcol - base.astype(jnp.float32)
        hit = col == jnp.concatenate([want] * (width // SB), axis=1)
        pick = jnp.sum(jnp.where(hit, logits, 0.0), axis=1, keepdims=True)
        lane = lax.broadcasted_iota(jnp.int32, (logits.shape[0], SB), 1)
        both = jnp.where(lane == 0, lse, jnp.where(lane == 1, pick, 0.0))
        return both.T[0:2]

    def do_a(xs, row):
        rows = pl.ds(row, RC)
        logits = jnp.dot(
            hh[xs, rows, :], wa[...].reshape(NX * NY * KLOC, QA), preferred_element_type=jnp.float32
        ) + pa[xs, rows, :].astype(jnp.float32)
        st[xs, 0:2, rows] = stats(logits, v_id * VLOC + x * QA, tt[xs, rows, :])

    def do_b(p, xs, row, partial):
        rows = pl.ds(row, RC)
        logits = jnp.dot(
            hh[xs, rows, :], wb[p].reshape(NX * NY * KLOC, QB), preferred_element_type=jnp.float32
        ) + partial.astype(jnp.float32)
        return stats(logits, v_id * VLOC + B0 + xp(2 * p) * QB, tt[xs, rows, :])

    for d in own_pa + own_pb:
        d.wait()
    none = lax.broadcasted_iota(jnp.int32, (2, ROWS), 0) == 0
    st[far, 2:4] = jnp.where(none, -1e30, 0.0)

    def sx_copy(r):
        to = lax.rem(x + NX - r, NX)
        return copy(st.at[to], sx.at[x], sx_s.at[NX - r], sx_r.at[NX - r], dev(x_=to))

    def part(j, carry):
        k = jnp.maximum(j - NRC, 0)
        i = jnp.where(j < NRC, j, lax.div(k, 3))
        r = jnp.where(j < NRC, 0, 1 + lax.rem(lax.rem(k, 3) + 1, 3))
        xs = lax.rem(x + NX - r, NX)
        row = pl.multiple_of(i * RC, RC)

        @pl.when(j >= NRC)
        def _():
            ref = pa.at[xs, pl.ds(row, RC)]
            copy(ref, ref, pa_s.at[r, i], pa_r.at[r, i], dev()).wait_recv()

        do_a(xs, row)

        @pl.when(j == NRC + 3 * (NRC - 1))
        def _():
            sx_copy(2).start()

        return carry

    def part_b(j, carry):
        k = jnp.maximum(j - NRC, 0)
        i = jnp.where(j < NRC, j, lax.div(k, 2))
        r = jnp.where(j < NRC, 0, 1 + 2 * lax.rem(k, 2))
        xs = lax.rem(x + NX - r, NX)
        row = pl.multiple_of(i * RC, RC)

        @pl.when(j >= NRC)
        def _():
            ref = pb.at[xs, pl.ds(row, RC)]
            copy(ref, ref, pb_s.at[r, i], pb_r.at[r, i], dev()).wait_recv()

        st[xs, 2:4, pl.ds(row, RC)] = do_b(0, xs, row, pb[xs, pl.ds(row, RC), :])

        @pl.when(j >= NRC + 2 * (NRC - 1))
        def _():
            sx_copy(r).start()

        return carry

    def part_c(i, carry):
        row = pl.multiple_of(i * RC, RC)
        stb[:, pl.ds(row, RC)] = do_b(1, x, row, pc[pl.ds(row, RC), :])
        return carry

    lax.fori_loop(0, NRC, part, 0)
    pass_yb(0, 2)
    lax.fori_loop(NRC, NRC + 3, part, 0)
    pass_yb(1, 2)
    lax.fori_loop(NRC + 3, NRC + 3 * NRC, part, 0)
    wait_yb(0, 2)
    lax.fori_loop(0, NRC + 2 * NRC, part_b, 0)
    n_early = len(sends)
    sends.extend(sx_copy(r) for r in order)
    sx[x] = st[x]
    wait_yb(1, 2)
    lax.fori_loop(0, NRC, part_c, 0)
    for d in sends[:n_early]:
        d.wait_send()
    for s in range(3):
        for r in range(NX):
            cu, cd = ya_pass(s, r)

            @pl.when(go_up(s))
            def _():
                cu.wait_send()

            @pl.when(go_down(s))
            def _():
                cd.wait_send()

        for p in range(2):
            bu, bd = yb_pass(p, s)

            @pl.when(go_up(s))
            def _():
                bu.wait_send()

            @pl.when(go_down(s))
            def _():
                bd.wait_send()

    for r in order:
        ref = sx.at[xm(r)]
        copy(ref, ref, sx_s.at[r], sx_r.at[r], dev()).wait_recv()

    mine = sx[...]
    extra = stb[...]
    lses = jnp.concatenate([mine[:, 0, :], mine[:, 2, :]], axis=0)
    top = jnp.maximum(jnp.max(lses, axis=0, keepdims=True), extra[0:1])
    total = jnp.sum(jnp.exp(lses - top), axis=0, keepdims=True) + jnp.exp(extra[0:1] - top)
    lse = top + jnp.log(total)
    pick = jnp.sum(mine[:, 1, :] + mine[:, 3, :], axis=0, keepdims=True) + extra[1:2]
    sv[v_id, 0:1] = lse
    sv[v_id, 1:2] = pick

    def peer(i, sign):
        dz = (4, 3, 5, 2, 6, 1, 7, 0)[i // 4]
        return (
            lax.rem(yh + 1 - i % 4 // 2, 2), lax.rem(z + NZ + sign * dz, NZ), lax.rem(c + 1 - i % 2, 2)
        )

    for i in range(31):
        to = peer(i, 1)
        start(copy(sv.at[v_id], sv.at[v_id], sv_s.at[i], sv_r.at[i], dev(yh_=to[0], z_=to[1], c_=to[2])))
    for d in sends[n_early:]:
        d.wait_send()
    for i in range(30, -1, -1):
        a_, b_, c_ = peer(i, -1)
        ref = sv.at[a_ * 16 + b_ * 2 + c_]
        copy(ref, ref, sv_s.at[i], sv_r.at[i], dev()).wait_recv()
    every = sv[...]
    lses, picks = every[:, 0, :], every[:, 1, :]
    top = jnp.max(lses, axis=0, keepdims=True)
    total = jnp.sum(jnp.exp(lses - top), axis=0, keepdims=True)
    out_ref[...] = top + jnp.log(total) - jnp.sum(picks, axis=0, keepdims=True)


def on_device(hidden, weight_values, scales, partial_logits, targets):
    vmem = pl.BlockSpec(memory_space=pltpu.VMEM)
    dma = pltpu.SemaphoreType.DMA
    bf, f32 = jnp.bfloat16, jnp.float32
    n = NX * NY
    loss = pl.pallas_call(
        kernel,
        out_shape=jax.ShapeDtypeStruct((1, ROWS), f32),
        in_specs=[pl.BlockSpec(memory_space=pltpu.HBM)] * 5,
        out_specs=vmem,
        scratch_shapes=[
            pltpu.VMEM((KLOC, VLOC), bf),
            pltpu.VMEM((VLOC // SB, KLOC), f32),
            pltpu.VMEM((NX, KLOC, QA), bf),
            pltpu.VMEM((NX, KLOC, QB), bf),
            pltpu.VMEM((n, KLOC, QA), bf),
            pltpu.VMEM((2, n, KLOC, QB), bf),
            pltpu.VMEM((NX, 2, NZ, 2, KSH, ROWS), bf),
            pltpu.VMEM((NX, ROWS, n * KLOC), bf),
            pltpu.VMEM((NX, ROWS, QA), bf),
            pltpu.VMEM((NX, ROWS, QB), bf),
            pltpu.VMEM((ROWS, QB), bf),
            pltpu.VMEM((NX, 1, ROWS), jnp.int32),
            pltpu.VMEM((NX, ROWS, SB), f32),
            pltpu.VMEM((NX, 4, ROWS), f32),
            pltpu.VMEM((2, ROWS), f32),
            pltpu.VMEM((NX, 4, ROWS), f32),
            pltpu.VMEM((32, 2, ROWS), f32),
            dma((4,)),
            dma, dma, dma((4,)), dma((4,)), dma((2, 2, 2, 4)), dma((2, 2, 2, 4)), dma((2, 8)), dma((2, 8)),
            dma((4,)), dma((4,)), dma((2, 4)), dma((2, 4)),
            dma((2, 3, 4)), dma((2, 3, 4)), dma((2, 2, 3)), dma((2, 2, 3)),
            dma((4, NRC)), dma((4, NRC)), dma((4, NRC)), dma((4, NRC)), dma((NRC,)), dma((2,)),
            dma((4,)), dma((4,)), dma((4,)), dma((4,)), dma((31,)), dma((31,)),
        ],
        compiler_params=pltpu.CompilerParams(
            collective_id=0, has_side_effects=True, vmem_limit_bytes=60 << 20
        ),
    )(hidden.T, weight_values, scales.T, partial_logits, targets.reshape(1, ROWS))
    return loss.reshape(ROWS)


def solution(mesh):
    in_specs = (P("tok", "voc"), P("tok", "voc"), P("tok", "voc"), P("tok", "voc"), P("tok"))
    return jax.shard_map(on_device, mesh=mesh, in_specs=in_specs, out_specs=P("tok"), check_vma=False)
```

```python
import functools

import jax
import jax.numpy as jnp
from jax import lax
from jax.experimental import pallas as pl
from jax.experimental.pallas import tpu as pltpu
from jax.sharding import PartitionSpec as P

MESH = pl.DeviceIdType.MESH
NX, NY, NZ = 4, 4, 8
ROWS, KLOC, VLOC, KSH, SB = 512, 64, 4096, 32, 128
QG = 6
QA = QG * SB
BG = VLOC // SB // NX - QG
QB = BG * SB
B0 = NX * QA
RC = 256
NRC = ROWS // RC


def kernel(
    hid_ref, w_ref, sc_ref, part_ref, tgt_ref, out_ref,
    wv, scv, ws, wsb, wa, wb, ht, hh, pa, pb, pc, tg, tt, st, stb, sx, sv, in_l,
    hy_s, hy_r, hx_s, hx_r, z_s, z_r, c_s, c_r, wax_s, wax_r, wbx_s, wbx_r,
    ya_s, ya_r, yb_s, yb_r, pa_s, pa_r, pb_s, pb_r, pa_l, pb_l, tg_s, tg_r, sx_s, sx_r, sv_s, sv_r,
):
    t_id, v_id = lax.axis_index("tok"), lax.axis_index("voc")
    x, y = lax.rem(t_id, NX), lax.div(t_id, NX)
    yh, z, c = lax.div(v_id, 16), lax.rem(lax.div(v_id, 2), NZ), lax.rem(v_id, 2)

    def dev(x_=None, y_=None, yh_=None, z_=None, c_=None):
        x_, y_ = x if x_ is None else x_, y if y_ is None else y_
        yh_, z_, c_ = yh if yh_ is None else yh_, z if z_ is None else z_, c if c_ is None else c_
        return (y_ * NX + x_, yh_ * 16 + z_ * 2 + c_)

    def xp(r):
        return lax.rem(x + r, NX)

    def xm(r):
        return lax.rem(x + NX - r, NX)

    def copy(src, dst, ss, rs, to):
        return pltpu.make_async_remote_copy(
            src_ref=src, dst_ref=dst, send_sem=ss, recv_sem=rs, device_id=to, device_id_type=MESH
        )

    bar = pltpu.get_barrier_semaphore()

    def greet(to):
        pl.semaphore_signal(bar, inc=1, device_id=to, device_id_type=MESH)

    for r in range(1, NX):
        greet(dev(x_=xp(r)))
    for r in range(1, NZ):
        greet(dev(z_=lax.rem(z + r, NZ)))
    for r in range(1, 4):
        greet(dev(yh_=lax.rem(yh + r // 2, 2), c_=lax.rem(c + r % 2, 2)))

    @pl.when(y > 0)
    def _():
        greet(dev(y_=y - 1))

    @pl.when(y < NY - 1)
    def _():
        greet(dev(y_=y + 1))

    loads = [
        pltpu.make_async_copy(w_ref, wv, in_l.at[0]),
        pltpu.make_async_copy(sc_ref, scv, in_l.at[1]),
        pltpu.make_async_copy(hid_ref, ht.at[x, yh, z, c], in_l.at[2]),
        pltpu.make_async_copy(tgt_ref, tg.at[x], in_l.at[3]),
    ]
    for d in loads:
        d.start()
    own_pa = [
        pltpu.make_async_copy(
            part_ref.at[pl.ds(i * RC, RC), pl.ds(pl.multiple_of(x * QA, SB), QA)],
            pa.at[x, pl.ds(i * RC, RC)], pa_l.at[i],
        )
        for i in range(NRC)
    ]
    for d in own_pa:
        d.start()
    far = xp(2)
    own_pb = [
        pltpu.make_async_copy(
            part_ref.at[:, pl.ds(pl.multiple_of(B0 + q * QB, SB), QB)], dst, pb_l.at[i]
        )
        for i, (q, dst) in enumerate(((x, pb.at[x]), (far, pc)))
    ]
    for d in own_pb:
        d.start()

    near = jnp.where(y > 0, 1, 0) + jnp.where(y < NY - 1, 1, 0)
    pl.semaphore_wait(bar, (NX - 1) + (NZ - 1) + 3 + near)
    loads[2].wait()

    sends = []

    def start(d):
        d.start()
        sends.append(d)

    def hx(r):
        ref = ht.at[x, yh, z, c]
        return copy(ref, ref, hx_s.at[r], hx_r.at[r], dev(x_=xp(r)))

    def hx_wait(r):
        ref = ht.at[xm(r), yh, z, c]
        copy(ref, ref, hx_s.at[r], hx_r.at[r], dev(x_=xp(r))).wait_recv()

    order = (1, 3, 2)

    def ya_pass(s, r):
        xs = xm(r)
        up = wa.at[jnp.maximum(y - s, 0) * NX + xs]
        down = wa.at[jnp.minimum(y + s, NY - 1) * NX + xs]
        cu = copy(up, up, ya_s.at[0, s, r], ya_r.at[0, s, r], dev(y_=jnp.minimum(y + 1, NY - 1)))
        cd = copy(down, down, ya_s.at[1, s, r], ya_r.at[1, s, r], dev(y_=jnp.maximum(y - 1, 0)))
        return cu, cd

    def go_up(s):
        return jnp.logical_and(y < NY - 1, y >= s)

    def go_down(s):
        return jnp.logical_and(y > 0, y + s <= NY - 1)

    def send_ya(s, r):
        cu, cd = ya_pass(s, r)

        @pl.when(go_up(s))
        def _():
            cu.start()

        @pl.when(go_down(s))
        def _():
            cd.start()

    def wait_ya(s, r):
        xs = xm(r)
        lo = wa.at[jnp.maximum(y - s - 1, 0) * NX + xs]
        hi = wa.at[jnp.minimum(y + s + 1, NY - 1) * NX + xs]

        @pl.when(y >= s + 1)
        def _():
            copy(lo, lo, ya_s.at[0, s, r], ya_r.at[0, s, r], dev()).wait_recv()

        @pl.when(y + s + 1 <= NY - 1)
        def _():
            copy(hi, hi, ya_s.at[1, s, r], ya_r.at[1, s, r], dev()).wait_recv()

    def yb_pass(p, s):
        up = wb.at[p, pl.ds(jnp.maximum(y - s, 0) * NX, NX)]
        down = wb.at[p, pl.ds(jnp.minimum(y + s, NY - 1) * NX, NX)]
        cu = copy(up, up, yb_s.at[p, 0, s], yb_r.at[p, 0, s], dev(y_=jnp.minimum(y + 1, NY - 1)))
        cd = copy(down, down, yb_s.at[p, 1, s], yb_r.at[p, 1, s], dev(y_=jnp.maximum(y - 1, 0)))
        return cu, cd

    def send_yb(p, s):
        cu, cd = yb_pass(p, s)

        @pl.when(go_up(s))
        def _():
            cu.start()

        @pl.when(go_down(s))
        def _():
            cd.start()

    def wait_yb(p, s):
        lo = wb.at[p, pl.ds(jnp.maximum(y - s - 1, 0) * NX, NX)]
        hi = wb.at[p, pl.ds(jnp.minimum(y + s + 1, NY - 1) * NX, NX)]

        @pl.when(y >= s + 1)
        def _():
            copy(lo, lo, yb_s.at[p, 0, s], yb_r.at[p, 0, s], dev()).wait_recv()

        @pl.when(y + s + 1 <= NY - 1)
        def _():
            copy(hi, hi, yb_s.at[p, 1, s], yb_r.at[p, 1, s], dev()).wait_recv()

    def zblock(stream, b):
        return ht.at[:, yh if stream == 0 else 1 - yh, b, c]

    def zhalf(stream, h, b):
        return ht.at[2 * h:2 * h + 2, yh if stream == 0 else 1 - yh, b, c]

    def zcopy(stream, h, way, k, b, to):
        ref = zhalf(stream, h, b)
        return copy(ref, ref, z_s.at[stream, h, way, k], z_r.at[stream, h, way, k], to)

    def send_c(stream, j, b):
        ref = zblock(stream, b)
        start(copy(ref, ref, c_s.at[stream, j], c_r.at[stream, j], dev(c_=1 - c)))

    def send_z(stream, k):
        up, down = lax.rem(z + NZ - k, NZ), lax.rem(z + k, NZ)
        for h in range(2):
            if k < 4 - h:
                start(zcopy(stream, h, 0, k, up, dev(z_=lax.rem(z + 1, NZ))))
            if k < 3 + h:
                start(zcopy(stream, h, 1, k, down, dev(z_=lax.rem(z + NZ - 1, NZ))))
        send_c(stream, k, up)
        if 0 < k < 4:
            send_c(stream, 4 + k, down)

    def step_z(stream, k):
        up, down = lax.rem(z + NZ - k - 1, NZ), lax.rem(z + k + 1, NZ)
        for h in range(2):
            if k < 4 - h:
                zcopy(stream, h, 0, k, up, dev()).wait_recv()
            if k < 3 + h:
                zcopy(stream, h, 1, k, down, dev()).wait_recv()
        if k < 3:
            send_z(stream, k + 1)
        else:
            send_c(stream, 4, up)

    def wait_c(stream):
        for j in range(NZ):
            b = lax.rem(z + NZ - j, NZ) if j <= 4 else lax.rem(z + j - 4, NZ)
            ref = ht.at[:, yh if stream == 0 else 1 - yh, b, 1 - c]
            copy(ref, ref, c_s.at[stream, j], c_r.at[stream, j], dev()).wait_recv()

    def pa_copy(r, i):
        src = part_ref.at[pl.ds(i * RC, RC), pl.ds(pl.multiple_of(xp(r) * QA, SB), QA)]
        return copy(src, pa.at[x, pl.ds(i * RC, RC)], pa_s.at[r, i], pa_r.at[r, i], dev(x_=xp(r)))

    def pb_copy(r, i):
        src = part_ref.at[pl.ds(i * RC, RC), pl.ds(pl.multiple_of(B0 + xp(r) * QB, SB), QB)]
        return copy(src, pb.at[x, pl.ds(i * RC, RC)], pb_s.at[r, i], pb_r.at[r, i], dev(x_=xp(r)))

    def wbx_wait(p):
        for r in order:
            ref = wb.at[p, y * NX + xm(r)]
            copy(ref, ref, wbx_s.at[p, r], wbx_r.at[p, r], dev()).wait_recv()

    def wax_wait(r):
        ref = wa.at[y * NX + xm(r)]
        copy(ref, ref, wax_s.at[r], wax_r.at[r], dev()).wait_recv()

    def turn(stream):
        half = yh if stream == 0 else 1 - yh

        def one(i, carry):
            for kb in range(4):
                blk = ht[i, half, kb * 2:kb * 2 + 2].reshape(SB, ROWS)
                hh[i, :, pl.ds(pl.multiple_of(half * 4 * SB, SB) + kb * SB, SB)] = blk.T
            return carry

        lax.fori_loop(0, NX, one, 0)

    def send_wb(p):
        for r in order:
            start(copy(wsb.at[xp(r + 2 * p)], wb.at[p, t_id], wbx_s.at[p, r], wbx_r.at[p, r], dev(x_=xp(r))))

    def pass_ya(s, r):
        wait_ya(s - 1, r)
        send_ya(s, r)

    def pass_yb(p, s):
        wait_yb(p, s - 1)
        send_yb(p, s)

    for r in order:
        start(hx(r))

    for i in (0, 1, 3):
        loads[i].wait()
    sc = scv[...].T

    def dense(g):
        scaled = wv[:, g * SB:(g + 1) * SB].astype(jnp.float32) * sc[:, g:g + 1]
        return scaled.astype(jnp.bfloat16)

    for q in range(NX):
        for g in range(QG):
            ws[q, :, g * SB:(g + 1) * SB] = dense(q * QG + g)
        for g in range(BG):
            wsb[q, :, g * SB:(g + 1) * SB] = dense(NX * QG + q * BG + g)
    wa[t_id] = ws[x]
    wb[0, t_id] = wsb[x]
    wb[1, t_id] = wsb[far]

    send_ya(0, 0)
    for r in order:
        start(copy(ws.at[xp(r)], wa.at[t_id], wax_s.at[r], wax_r.at[r], dev(x_=xp(r))))
    send_wb(0)
    send_wb(1)
    for r in order:
        start(copy(tg.at[x], tg.at[x], tg_s.at[r], tg_r.at[r], dev(x_=xp(r))))
    for i in range(NRC):
        for r in (2, 1, 3):
            start(pa_copy(r, i))
    for i in range(NRC):
        for r in (1, 3):
            start(pb_copy(r, i))
    for r in order:
        hx_wait(r)
    send_z(0, 0)
    ref = zblock(0, z)
    start(copy(ref, ref, hy_s, hy_r, dev(yh_=1 - yh)))
    wax_wait(1)
    send_ya(0, 1)
    wax_wait(3)
    send_ya(0, 3)
    pass_ya(1, 0)
    wax_wait(2)
    send_ya(0, 2)
    step_z(0, 0)
    ref = zblock(1, z)
    copy(ref, ref, hy_s, hy_r, dev()).wait_recv()
    send_z(1, 0)
    pass_ya(1, 1)
    pass_ya(2, 0)
    pass_ya(1, 3)
    pass_ya(1, 2)
    step_z(0, 1)
    wbx_wait(0)
    send_yb(0, 0)
    step_z(1, 0)
    pass_ya(2, 1)
    pass_ya(2, 3)
    step_z(0, 2)
    pass_ya(2, 2)
    step_z(1, 1)
    wbx_wait(1)
    send_yb(1, 0)
    step_z(0, 3)
    step_z(1, 2)
    pass_yb(0, 1)

    for r in order:
        ref = tg.at[xm(r)]
        copy(ref, ref, tg_s.at[r], tg_r.at[r], dev()).wait_recv()

    def spread(i, carry):
        row = tg[i].astype(jnp.float32)
        tt[i] = jnp.broadcast_to(row, (SB, ROWS)).T
        return carry

    lax.fori_loop(0, NX, spread, 0)
    wait_c(0)
    turn(0)
    step_z(1, 3)
    pass_yb(1, 1)
    wait_c(1)
    turn(1)
    for r in (0, 1, 3, 2):
        wait_ya(2, r)

    def stats(logits, base, tcol):
        width = logits.shape[1]
        top = jnp.max(logits, axis=1, keepdims=True)
        lse = top + jnp.log(jnp.sum(jnp.exp(logits - top), axis=1, keepdims=True))
        col = lax.broadcasted_iota(jnp.int32, logits.shape, 1).astype(jnp.float32)
        want = tcol - base.astype(jnp.float32)
        hit = col == jnp.concatenate([want] * (width // SB), axis=1)
        pick = jnp.sum(jnp.where(hit, logits, 0.0), axis=1, keepdims=True)
        lane = lax.broadcasted_iota(jnp.int32, (logits.shape[0], SB), 1)
        both = jnp.where(lane == 0, lse, jnp.where(lane == 1, pick, 0.0))
        return both.T[0:2]

    def do_a(xs, row):
        rows = pl.ds(row, RC)
        logits = jnp.dot(
            hh[xs, rows, :], wa[...].reshape(NX * NY * KLOC, QA), preferred_element_type=jnp.float32
        ) + pa[xs, rows, :].astype(jnp.float32)
        st[xs, 0:2, rows] = stats(logits, v_id * VLOC + x * QA, tt[xs, rows, :])

    def do_b(p, xs, row, partial):
        rows = pl.ds(row, RC)
        logits = jnp.dot(
            hh[xs, rows, :], wb[p].reshape(NX * NY * KLOC, QB), preferred_element_type=jnp.float32
        ) + partial.astype(jnp.float32)
        return stats(logits, v_id * VLOC + B0 + xp(2 * p) * QB, tt[xs, rows, :])

    for d in own_pa + own_pb:
        d.wait()
    none = lax.broadcasted_iota(jnp.int32, (2, ROWS), 0) == 0
    st[far, 2:4] = jnp.where(none, -1e30, 0.0)

    def sx_copy(r):
        to = lax.rem(x + NX - r, NX)
        return copy(st.at[to], sx.at[x], sx_s.at[NX - r], sx_r.at[NX - r], dev(x_=to))

    def part(j, carry):
        k = jnp.maximum(j - NRC, 0)
        i = jnp.where(j < NRC, j, lax.div(k, 3))
        r = jnp.where(j < NRC, 0, 1 + lax.rem(lax.rem(k, 3) + 1, 3))
        xs = lax.rem(x + NX - r, NX)
        row = pl.multiple_of(i * RC, RC)

        @pl.when(j >= NRC)
        def _():
            ref = pa.at[xs, pl.ds(row, RC)]
            copy(ref, ref, pa_s.at[r, i], pa_r.at[r, i], dev()).wait_recv()

        do_a(xs, row)

        @pl.when(j == NRC + 3 * (NRC - 1))
        def _():
            sx_copy(2).start()

        return carry

    def part_b(j, carry):
        own = j >= 2 * NRC
        i = jnp.where(own, j - 2 * NRC, lax.div(j, 2))
        r = jnp.where(own, 0, 1 + 2 * lax.rem(j, 2))
        xs = lax.rem(x + NX - r, NX)
        row = pl.multiple_of(i * RC, RC)

        @pl.when(j < 2 * NRC)
        def _():
            ref = pb.at[xs, pl.ds(row, RC)]
            copy(ref, ref, pb_s.at[r, i], pb_r.at[r, i], dev()).wait_recv()

        st[xs, 2:4, pl.ds(row, RC)] = do_b(0, xs, row, pb[xs, pl.ds(row, RC), :])

        @pl.when(jnp.logical_and(j >= 2 * (NRC - 1), j < 2 * NRC))
        def _():
            sx_copy(r).start()

        return carry

    def part_c(i, carry):
        row = pl.multiple_of(i * RC, RC)
        stb[:, pl.ds(row, RC)] = do_b(1, x, row, pc[pl.ds(row, RC), :])
        return carry

    lax.fori_loop(0, NRC, part, 0)
    pass_yb(0, 2)
    lax.fori_loop(NRC, NRC + 3, part, 0)
    pass_yb(1, 2)
    lax.fori_loop(NRC + 3, NRC + 3 * NRC, part, 0)
    wait_yb(0, 2)
    lax.fori_loop(0, NRC + 2 * NRC, part_b, 0)
    n_early = len(sends)
    sends.extend(sx_copy(r) for r in order)
    sx[x] = st[x]
    wait_yb(1, 2)
    lax.fori_loop(0, NRC, part_c, 0)
    for d in sends[:n_early]:
        d.wait_send()
    for s in range(3):
        for r in range(NX):
            cu, cd = ya_pass(s, r)

            @pl.when(go_up(s))
            def _():
                cu.wait_send()

            @pl.when(go_down(s))
            def _():
                cd.wait_send()

        for p in range(2):
            bu, bd = yb_pass(p, s)

            @pl.when(go_up(s))
            def _():
                bu.wait_send()

            @pl.when(go_down(s))
            def _():
                bd.wait_send()

    for r in order:
        ref = sx.at[xm(r)]
        copy(ref, ref, sx_s.at[r], sx_r.at[r], dev()).wait_recv()

    mine = sx[...]
    extra = stb[...]
    lses = jnp.concatenate([mine[:, 0, :], mine[:, 2, :]], axis=0)
    top = jnp.maximum(jnp.max(lses, axis=0, keepdims=True), extra[0:1])
    total = jnp.sum(jnp.exp(lses - top), axis=0, keepdims=True) + jnp.exp(extra[0:1] - top)
    lse = top + jnp.log(total)
    pick = jnp.sum(mine[:, 1, :] + mine[:, 3, :], axis=0, keepdims=True) + extra[1:2]
    sv[v_id, 0:1] = lse
    sv[v_id, 1:2] = pick

    def peer(i, sign):
        dz = (4, 3, 5, 2, 6, 1, 7, 0)[i // 4]
        return (
            lax.rem(yh + 1 - i % 4 // 2, 2), lax.rem(z + NZ + sign * dz, NZ), lax.rem(c + 1 - i % 2, 2)
        )

    for i in range(31):
        to = peer(i, 1)
        start(copy(sv.at[v_id], sv.at[v_id], sv_s.at[i], sv_r.at[i], dev(yh_=to[0], z_=to[1], c_=to[2])))
    for d in sends[n_early:]:
        d.wait_send()
    for i in range(30, -1, -1):
        a_, b_, c_ = peer(i, -1)
        ref = sv.at[a_ * 16 + b_ * 2 + c_]
        copy(ref, ref, sv_s.at[i], sv_r.at[i], dev()).wait_recv()
    every = sv[...]
    lses, picks = every[:, 0, :], every[:, 1, :]
    top = jnp.max(lses, axis=0, keepdims=True)
    total = jnp.sum(jnp.exp(lses - top), axis=0, keepdims=True)
    out_ref[...] = top + jnp.log(total) - jnp.sum(picks, axis=0, keepdims=True)


def on_device(hidden, weight_values, scales, partial_logits, targets):
    vmem = pl.BlockSpec(memory_space=pltpu.VMEM)
    dma = pltpu.SemaphoreType.DMA
    bf, f32 = jnp.bfloat16, jnp.float32
    n = NX * NY
    loss = pl.pallas_call(
        kernel,
        out_shape=jax.ShapeDtypeStruct((1, ROWS), f32),
        in_specs=[pl.BlockSpec(memory_space=pltpu.HBM)] * 5,
        out_specs=vmem,
        scratch_shapes=[
            pltpu.VMEM((KLOC, VLOC), bf),
            pltpu.VMEM((VLOC // SB, KLOC), f32),
            pltpu.VMEM((NX, KLOC, QA), bf),
            pltpu.VMEM((NX, KLOC, QB), bf),
            pltpu.VMEM((n, KLOC, QA), bf),
            pltpu.VMEM((2, n, KLOC, QB), bf),
            pltpu.VMEM((NX, 2, NZ, 2, KSH, ROWS), bf),
            pltpu.VMEM((NX, ROWS, n * KLOC), bf),
            pltpu.VMEM((NX, ROWS, QA), bf),
            pltpu.VMEM((NX, ROWS, QB), bf),
            pltpu.VMEM((ROWS, QB), bf),
            pltpu.VMEM((NX, 1, ROWS), jnp.int32),
            pltpu.VMEM((NX, ROWS, SB), f32),
            pltpu.VMEM((NX, 4, ROWS), f32),
            pltpu.VMEM((2, ROWS), f32),
            pltpu.VMEM((NX, 4, ROWS), f32),
            pltpu.VMEM((32, 2, ROWS), f32),
            dma((4,)),
            dma, dma, dma((4,)), dma((4,)), dma((2, 2, 2, 4)), dma((2, 2, 2, 4)), dma((2, 8)), dma((2, 8)),
            dma((4,)), dma((4,)), dma((2, 4)), dma((2, 4)),
            dma((2, 3, 4)), dma((2, 3, 4)), dma((2, 2, 3)), dma((2, 2, 3)),
            dma((4, NRC)), dma((4, NRC)), dma((4, NRC)), dma((4, NRC)), dma((NRC,)), dma((2,)),
            dma((4,)), dma((4,)), dma((4,)), dma((4,)), dma((31,)), dma((31,)),
        ],
        compiler_params=pltpu.CompilerParams(
            collective_id=0, has_side_effects=True, vmem_limit_bytes=60 << 20
        ),
    )(hidden.T, weight_values, scales.T, partial_logits, targets.reshape(1, ROWS))
    return loss.reshape(ROWS)


def solution(mesh):
    in_specs = (P("tok", "voc"), P("tok", "voc"), P("tok", "voc"), P("tok", "voc"), P("tok"))
    return jax.shard_map(on_device, mesh=mesh, in_specs=in_specs, out_specs=P("tok"), check_vma=False)
```
